32 devices in a mesh: blk: 16 (over z, y, x), seg: 2 (over core).
Axes of the slice: x: 2, y: 2, z: 4, core: 2. Of those that a mesh axis runs over, the one named last changes fastest.
Arguments:
- spectra: bfloat16 [28, 2048, 2, 512], P('seg', 'blk'), as said below
- valid_flags: int32 [28, 2048], P('seg', 'blk'), may hold values 0 or 1
Outputs:
- correlations: bfloat16 [2, 2048, 128, 1024], P(None, ('blk', 'seg'))
The draws below stay inside these ranges and needn't reach their ends.
Inputs may be any that keep to these rules, and one draw needn't show every extreme that they name: `spectra`: rough spectral values; their scale varies from bin to bin, channel to channel and window to window.
All inputs are finite; a program needn't handle non-finite values. No bound on the sum of `valid_flags` on one device may be relied on, other than what follows from the above.
Results may differ from the reference program's by a relative error of at most 0.015.
Values may be sent and summed in bfloat16 or wider, within the bound.
A program may use at most 192 MiB of HBM per device.

```python
import math
import jax
import jax.numpy as jnp
from jax import lax

CHANNELS = 2048
FREQ_BINS = 512
LAG_COUNT = 1024
WIN_SAMPLES = 15000
BAND_START = 30
SMOOTH_HALF = 32
ROUNDS = 2
WIN_DEV = 14
WINDOWS = 28
N_BLK = 16
N_SEG = 2


def draw_spectra(key, part):
    key_base, key_bins, key_traces = jax.random.split(key, 3)
    full_shape = (WINDOWS, CHANNELS, 2, FREQ_BINS)
    base_draw = jax.random.truncated_normal(key_base, -5.0, 5.0, full_shape, jnp.float32)
    trace_span = math.log(10.0)
    bin_scale = jnp.exp(jax.random.uniform(key_bins, (1, CHANNELS, 1, FREQ_BINS), jnp.float32, 0.0, math.log(10.0)))
    trace_scale = jnp.exp(jax.random.uniform(key_traces, (WINDOWS, CHANNELS, 1, 1), jnp.float32, 0.0, trace_span))
    return (base_draw * bin_scale * trace_scale).astype(jnp.bfloat16)


def touch_ends(array, key, smallest, top_value):
    longest = array.shape.index(max(array.shape))
    spots = []
    for shift in (0, 1):
        where = [jax.random.randint(jax.random.fold_in(key, axis), (), 0, length) for axis, length in enumerate(array.shape)]
        where[longest] = (where[longest] + shift) % array.shape[longest]
        spots.append(tuple(where))
    return array.at[spots[0]].set(smallest).at[spots[1]].set(top_value)


def setup_inputs(seed: int = 0) -> dict:
    streams_of = jax.random.split(jax.random.key(seed), 3)
    return {
        "spectra": draw_spectra(jax.random.fold_in(streams_of[2], 71), 0),
        "valid_flags": touch_ends((jax.random.randint(streams_of[1], (WINDOWS, CHANNELS), 0, 8) < 7).astype(jnp.int32), jax.random.fold_in(streams_of[1], 1), 0, 1),
    }


def lag_table(bin_count, lag_count):
    freq_ids = lax.broadcasted_iota(jnp.int32, (bin_count, lag_count), 0) + BAND_START
    delay_ids = lax.broadcasted_iota(jnp.int32, (bin_count, lag_count), 1) - lag_count // 2
    angles = jnp.mod(freq_ids * delay_ids, WIN_SAMPLES).astype(jnp.float32) * (2.0 * math.pi / WIN_SAMPLES)
    return jnp.stack([jnp.cos(angles), -jnp.sin(angles)], axis=1).astype(jnp.bfloat16)

def smooth_sum(values):
    bin_count = values.shape[-1]
    widths = [(0, 0)] * (values.ndim - 1) + [(SMOOTH_HALF, SMOOTH_HALF)]
    padded = jnp.pad(values, widths)
    total = jnp.zeros_like(values)
    for offset in range(2 * SMOOTH_HALF + 1):
        total = total + padded[..., offset:offset + bin_count]
    return total

def whiten_block(spectra_block, flags_block):
    real_part = spectra_block[:, :, 0, :].astype(jnp.float32)
    imag_part = spectra_block[:, :, 1, :].astype(jnp.float32)
    amplitude = jnp.sqrt(real_part * real_part + imag_part * imag_part).astype(jnp.bfloat16)
    amplitude_wide = lax.optimization_barrier(amplitude).astype(jnp.float32)
    counts = smooth_sum(jnp.ones((FREQ_BINS,), jnp.float32))
    smooth = smooth_sum(amplitude_wide) / counts
    scaling = flags_block.astype(jnp.float32)[:, :, None] / (smooth + 1e-05)
    return (spectra_block.astype(jnp.float32) * scaling[:, :, None, :]).astype(jnp.bfloat16)

def reference(spectra, valid_flags):
    block_width = CHANNELS // N_BLK
    block_ids = jnp.arange(N_BLK, dtype=jnp.int32)

    def whiten_one(block_id):
        start = (block_id * block_width).astype(jnp.int32)
        piece = lax.dynamic_slice_in_dim(spectra, start, block_width, 1)
        flags_piece = lax.dynamic_slice_in_dim(valid_flags, start, block_width, 1)
        return whiten_block(piece, flags_piece)
    whitened_all = lax.map(whiten_one, block_ids)
    table = lax.optimization_barrier(lag_table(FREQ_BINS, LAG_COUNT)).astype(jnp.float32)
    scaling = 1.0 / math.sqrt(WINDOWS * FREQ_BINS)
    outputs = []
    for rounds_done in range(ROUNDS):

        def one_block(block_id):
            partner_id = jnp.mod(block_id - rounds_done - 1, N_BLK).astype(jnp.int32)
            owned = whitened_all[block_id].astype(jnp.float32).reshape(N_SEG, WIN_DEV, block_width, 2, FREQ_BINS)
            partner = whitened_all[partner_id].astype(jnp.float32).reshape(N_SEG, WIN_DEV, block_width, 2, FREQ_BINS)
            rotated = jnp.stack([-partner[:, :, :, 1, :], partner[:, :, :, 0, :]], axis=3)
            stacked = jnp.stack([partner, rotated], axis=0)
            partials = jnp.einsum('swicf,kswjcf->sfikj', owned, stacked)
            rounded = lax.optimization_barrier(partials.astype(jnp.bfloat16)).astype(jnp.float32)
            stack = lax.optimization_barrier(jnp.sum(rounded, axis=0)).astype(jnp.bfloat16)
            stack_wide = lax.optimization_barrier(stack).astype(jnp.float32)
            result = jnp.einsum('fikj,fkl->ijl', stack_wide, table) * scaling
            return result.astype(jnp.bfloat16)
        per_block = lax.map(one_block, block_ids)
        outputs.append(per_block.reshape(CHANNELS, block_width, LAG_COUNT))
    return jnp.stack(outputs)
```

```python
import functools
import math

import jax
import jax.numpy as jnp
from jax import lax
from jax.experimental import pallas as pl
from jax.experimental.pallas import tpu as pltpu
from jax.sharding import PartitionSpec as P

LAG_COUNT = 1024
WIN_SAMPLES = 15000
BAND_START = 30
SMOOTH_HALF = 32
ROUNDS = 2


def passed_along(value, axis, steps):
    count = lax.axis_size(axis)
    pairs = [(source, (source + steps) % count) for source in range(count)]
    return lax.ppermute(value, axis, pairs)


def lag_table(bin_count, lag_count):
    freq_ids = lax.broadcasted_iota(jnp.int32, (bin_count, lag_count), 0) + BAND_START
    delay_ids = lax.broadcasted_iota(jnp.int32, (bin_count, lag_count), 1) - lag_count // 2
    angles = jnp.mod(freq_ids * delay_ids, WIN_SAMPLES).astype(jnp.float32) * (
        2.0 * math.pi / WIN_SAMPLES
    )
    return jnp.stack([jnp.cos(angles), -jnp.sin(angles)], axis=1).astype(jnp.bfloat16)


def whiten(spectra, valid_flags):
    bin_count = spectra.shape[3]
    real_part = spectra[:, :, 0, :].astype(jnp.float32)
    imag_part = spectra[:, :, 1, :].astype(jnp.float32)
    amplitude = jnp.sqrt(real_part * real_part + imag_part * imag_part).astype(jnp.bfloat16)
    row_ids = lax.broadcasted_iota(jnp.int32, (bin_count, bin_count), 0)
    col_ids = lax.broadcasted_iota(jnp.int32, (bin_count, bin_count), 1)
    band_mask = jnp.abs(row_ids - col_ids) <= SMOOTH_HALF
    counts = jnp.sum(band_mask.astype(jnp.float32), axis=0)
    summed = jnp.dot(
        amplitude.reshape(-1, bin_count),
        band_mask.astype(jnp.bfloat16),
        preferred_element_type=jnp.float32,
    )
    smooth = summed.reshape(amplitude.shape) / counts
    scaling = valid_flags.astype(jnp.float32)[:, :, None] / (smooth + 1e-05)
    whitened = (spectra.astype(jnp.float32) * scaling[:, :, None, :]).astype(jnp.bfloat16)
    return jnp.transpose(whitened, (3, 2, 0, 1))


def cross_terms(owned, partner):
    rotated = jnp.stack([-partner[:, 1], partner[:, 0]], axis=1)
    joined = jnp.concatenate([partner, rotated], axis=3)
    return lax.dot_general(
        owned, joined, (((1, 2), (1, 2)), ((0,), (0,))), preferred_element_type=jnp.float32
    )


def invert(received, table, scaling):
    bin_count, rows_here, doubled = received.shape
    stack = received.astype(jnp.bfloat16).reshape(bin_count, rows_here, 2, doubled // 2)
    result = lax.dot_general(
        stack, table, (((0, 2), (0, 1)), ((), ())), preferred_element_type=jnp.float32
    )
    return (result * scaling).astype(jnp.bfloat16)


def shards_plain(spectra, valid_flags):
    seg_count = lax.axis_size("seg")
    windows_here = spectra.shape[0]
    bin_count = spectra.shape[3]
    table = lag_table(bin_count, LAG_COUNT)
    scaling = 1.0 / math.sqrt(windows_here * seg_count * bin_count)
    owned = whiten(spectra, valid_flags)
    previous_white = owned
    results = []
    for rounds_done in range(ROUNDS):
        stride = rounds_done + 1
        previous_white = passed_along(owned, "blk", stride)
        partials = cross_terms(owned, previous_white)
        received = lax.psum_scatter(
            partials.astype(jnp.bfloat16), "seg", scatter_dimension=1, tiled=True
        ).astype(jnp.float32)
        results.append(invert(received, table, scaling))
    return jnp.stack(results)


PIECES = 8
ROW_GROUP = 4
MESH = pl.DeviceIdType.MESH


def exchange_kernel(blk_count, seg_count, own, gathered, own_all, transit, local_sem, near_send,
                    near_recv, seg_send, seg_recv):
    blk, seg = lax.axis_index("blk"), lax.axis_index("seg")
    place = lax.rem(blk, 4)
    low, high = lax.rem(place, 2), place // 2
    across_x = blk + 1 - 2 * low
    across_y = blk + 2 - 4 * high
    up_z = lax.rem(blk + 4, blk_count)
    down_z = lax.rem(blk + blk_count - 4, blk_count)
    siblings = [lax.rem(seg + k, seg_count) for k in range(1, seg_count)]
    bins = own.shape[0] // PIECES
    barrier = pltpu.get_barrier_semaphore()

    def greet(target_blk, target_seg):
        pl.semaphore_signal(barrier, inc=1, device_id=(target_blk, target_seg), device_id_type=MESH)

    greet(across_x, seg)
    greet(across_y, seg)
    for sibling in siblings:
        greet(blk, sibling)

    @pl.when(high == 1)
    def _():
        greet(up_z, seg)
        greet(down_z, seg)

    pl.semaphore_wait(barrier, 2 + len(siblings) + 2 * high)

    def part(k):
        return pl.ds(k * bins, bins)

    def near(src, dst, send_row, recv_row, k, target):
        return pltpu.make_async_remote_copy(
            src_ref=src, dst_ref=dst, send_sem=near_send.at[send_row, k],
            recv_sem=near_recv.at[recv_row, k], device_id=(target, seg), device_id_type=MESH)

    def own_x(k):
        return near(own.at[part(k)], gathered.at[0, seg, part(k)], 0, 0, k, across_x)

    def own_y(k):
        return near(own.at[part(k)], gathered.at[1, seg, part(k)], 1, 1, k, across_y)

    def own_z(k):
        return near(own.at[part(k)], transit.at[part(k)], 2, 2, k, up_z)

    def forward_y(k):
        return near(transit.at[part(k)], gathered.at[1, seg, part(k)], 3, 1, k, across_y)

    def forward_x(k):
        return near(gathered.at[1, seg, part(k)], gathered.at[0, seg, part(k)], 4, 0, k, across_x)

    def share(src, dst, row, k, n):
        return pltpu.make_async_remote_copy(
            src_ref=src, dst_ref=dst, send_sem=seg_send.at[row, k, n],
            recv_sem=seg_recv.at[row, k, n], device_id=(blk, siblings[n]), device_id_type=MESH)

    def share_round(r, k, n):
        piece = gathered.at[r, seg, part(k)]
        return share(piece, piece, r, k, n)

    def landed_round(r, k, n):
        piece = gathered.at[r, lax.rem(seg + seg_count - n - 1, seg_count), part(k)]
        return share(piece, piece, r, k, n)

    def share_own(k, n):
        return share(own.at[part(k)], own_all.at[seg, part(k)], 2, k, n)

    def landed_own(k, n):
        piece = own_all.at[lax.rem(seg + seg_count - n - 1, seg_count), part(k)]
        return share(piece, piece, 2, k, n)

    firsts = ((low == 0, own_x), (high == 0, own_y), (high == 1, own_z))

    def start_own(k):
        for condition, make in firsts:
            @pl.when(condition)
            def _(make=make):
                make(k).start()

    def wait_own(k):
        for condition, make in firsts:
            @pl.when(condition)
            def _(make=make):
                make(k).wait_send()

    start_own(0)
    start_own(1)
    local = pltpu.make_async_copy(own, own_all.at[seg], local_sem)
    local.start()
    for k in range(PIECES):
        for n in range(len(siblings)):
            share_own(k, n).start()
    for k in range(PIECES + 1):
        if k < PIECES:
            wait_own(k)
            if k + 2 < PIECES:
                start_own(k + 2)

            @pl.when(high == 1)
            def _():
                own_z(k).wait_recv()
                forward_y(k).start()

            own_y(k).wait_recv()

            @pl.when(low == 1)
            def _():
                forward_x(k).start()

            for n in range(len(siblings)):
                share_round(1, k, n).start()
        if k >= 1:
            own_x(k - 1).wait_recv()
            for n in range(len(siblings)):
                share_round(0, k - 1, n).start()
    for k in range(PIECES):
        @pl.when(high == 1)
        def _():
            forward_y(k).wait_send()

        @pl.when(low == 1)
        def _():
            forward_x(k).wait_send()

        for n in range(len(siblings)):
            for r in range(ROUNDS):
                share_round(r, k, n).wait_send()
                landed_round(r, k, n).wait_recv()
            share_own(k, n).wait_send()
            landed_own(k, n).wait_recv()
    local.wait()


def exchange(own, blk_count, seg_count):
    others = max(seg_count - 1, 1)
    anywhere = pl.BlockSpec(memory_space=pl.ANY)
    gathered, own_all, _ = pl.pallas_call(
        functools.partial(exchange_kernel, blk_count, seg_count),
        out_shape=(
            jax.ShapeDtypeStruct((ROUNDS, seg_count, *own.shape), own.dtype),
            jax.ShapeDtypeStruct((seg_count, *own.shape), own.dtype),
            jax.ShapeDtypeStruct(own.shape, own.dtype),
        ),
        in_specs=[anywhere],
        out_specs=(anywhere,) * 3,
        scratch_shapes=[
            pltpu.SemaphoreType.DMA,
            pltpu.SemaphoreType.DMA((5, PIECES)),
            pltpu.SemaphoreType.DMA((3, PIECES)),
            pltpu.SemaphoreType.DMA((3, PIECES, others)),
            pltpu.SemaphoreType.DMA((3, PIECES, others)),
        ],
        compiler_params=pltpu.CompilerParams(
            collective_id=0, has_side_effects=True, vmem_limit_bytes=60 * 2**20),
    )(own)
    return gathered, own_all


def correlate_kernel(chunk_count, scaling, own_ref, partner_ref, table_ref, out_ref, cross, left):
    step = pl.program_id(1)
    bins_here, rows, _ = own_ref.shape
    width = partner_ref.shape[-1]
    bin_count = cross.shape[1] // rows
    group = out_ref.shape[1]

    @pl.when(step < chunk_count)
    def _():
        @pl.loop(0, bins_here, unroll=8)
        def _(f):
            segments = partner_ref.shape[1]
            real = jnp.concatenate([partner_ref[0, s, f, 0] for s in range(segments)], axis=0)
            imag = jnp.concatenate([partner_ref[0, s, f, 1] for s in range(segments)], axis=0)
            joined = jnp.concatenate(
                [jnp.concatenate([real, -imag], axis=1), jnp.concatenate([imag, real], axis=1)], axis=0)
            result = jnp.dot(own_ref[f], joined, preferred_element_type=jnp.float32)
            start = pl.multiple_of((step * bins_here + f) * rows, 8)
            cross[0, pl.ds(start, rows), :] = result[:, :width]
            cross[1, pl.ds(start, rows), :] = result[:, width:]

    @pl.when(step >= chunk_count)
    def _():
        first = (step - chunk_count) * group
        for n in range(group):
            for k in range(2):
                picked = cross[k, pl.ds(first + n, bin_count, stride=rows), :]
                left[n * width:(n + 1) * width, k * bin_count:(k + 1) * bin_count] = (
                    picked.astype(jnp.bfloat16).T)
        lags = table_ref.shape[1]
        span = 256

        @pl.loop(0, lags // span, unroll=True)
        def _(c):
            columns = pl.ds(pl.multiple_of(c * span, span), span)
            result = jnp.dot(left[...], table_ref[:, columns], preferred_element_type=jnp.float32)
            out_ref[0, :, :, columns] = (result * scaling).astype(jnp.bfloat16).reshape(
                group, width, span)


def correlate(own, gathered, table, scaling):
    bin_count, rows, depth = own.shape
    rounds, seg_count, _, _, windows, width = gathered.shape
    lags = table.shape[1]
    bins_here = bin_count // 16
    chunk_count = bin_count // bins_here
    group = ROW_GROUP
    steps = chunk_count + rows // group
    return pl.pallas_call(
        functools.partial(correlate_kernel, chunk_count, scaling),
        grid=(rounds, steps),
        out_shape=jax.ShapeDtypeStruct((rounds, rows, width, lags), jnp.bfloat16),
        in_specs=[
            pl.BlockSpec((bins_here, rows, depth), lambda r, t: (jnp.minimum(t, chunk_count - 1), 0, 0)),
            pl.BlockSpec((1, seg_count, bins_here, 2, windows, width),
                         lambda r, t: (r, 0, jnp.minimum(t, chunk_count - 1), 0, 0, 0)),
            pl.BlockSpec((2 * bin_count, lags), lambda r, t: (0, 0)),
        ],
        out_specs=pl.BlockSpec((1, group, width, lags),
                               lambda r, t: (r, jnp.maximum(t - chunk_count, 0), 0, 0)),
        scratch_shapes=[
            pltpu.VMEM((2, bin_count * rows, width), jnp.float32),
            pltpu.VMEM((group * width, 2 * bin_count), jnp.bfloat16),
        ],
        compiler_params=pltpu.CompilerParams(vmem_limit_bytes=60 * 2**20),
        cost_estimate=pl.CostEstimate(
            flops=4 * rounds * rows * width * bin_count * lags,
            bytes_accessed=2 * rounds * rows * width * lags, transcendentals=0),
    )(own, gathered, table)


def shards(spectra, valid_flags):
    seg_count, blk_count = lax.axis_size("seg"), lax.axis_size("blk")
    windows_here, width, _, bin_count = spectra.shape
    rows = width // seg_count
    fits = 2 * bin_count * rows * width * 4 <= 36 * 2**20
    if width != 128 or rows % 8 or blk_count % 4 or blk_count < 8 or bin_count % 128 or not fits:
        return shards_plain(spectra, valid_flags)
    scaling = 1.0 / math.sqrt(windows_here * seg_count * bin_count)
    table = jnp.transpose(lag_table(bin_count, LAG_COUNT), (1, 0, 2)).reshape(2 * bin_count, LAG_COUNT)
    owned = whiten(spectra, valid_flags)
    padded = -(-windows_here // 16) * 16
    owned = jnp.pad(owned, ((0, 0), (0, 0), (0, padded - windows_here), (0, 0)))
    gathered, own_all = exchange(owned, blk_count, seg_count)
    mine = lax.dynamic_slice_in_dim(own_all, lax.axis_index("seg") * rows, rows, 4)
    mine = jnp.transpose(mine, (1, 4, 2, 0, 3)).reshape(bin_count, rows, 2 * seg_count * padded)
    return correlate(mine, gathered, table, scaling)


def solution(mesh):
    in_specs = (P("seg", "blk", None, None), P("seg", "blk"))
    out_specs = P(None, ("blk", "seg"), None, None)
    return jax.shard_map(shards, mesh=mesh, in_specs=in_specs, out_specs=out_specs, check_vma=False)
```

```python
import functools
import math

import jax
import jax.numpy as jnp
import numpy as np
from jax import lax
from jax.experimental import pallas as pl
from jax.experimental.pallas import tpu as pltpu
from jax.sharding import PartitionSpec as P

LAG_COUNT = 1024
WIN_SAMPLES = 15000
BAND_START = 30
SMOOTH_HALF = 32
ROUNDS = 2


def passed_along(value, axis, steps):
    count = lax.axis_size(axis)
    pairs = [(source, (source + steps) % count) for source in range(count)]
    return lax.ppermute(value, axis, pairs)


def lag_table(bin_count, lag_count):
    freq_ids = lax.broadcasted_iota(jnp.int32, (bin_count, lag_count), 0) + BAND_START
    delay_ids = lax.broadcasted_iota(jnp.int32, (bin_count, lag_count), 1) - lag_count // 2
    angles = jnp.mod(freq_ids * delay_ids, WIN_SAMPLES).astype(jnp.float32) * (
        2.0 * math.pi / WIN_SAMPLES
    )
    return jnp.stack([jnp.cos(angles), -jnp.sin(angles)], axis=1).astype(jnp.bfloat16)


def whiten(spectra, valid_flags):
    bin_count = spectra.shape[3]
    real_part = spectra[:, :, 0, :].astype(jnp.float32)
    imag_part = spectra[:, :, 1, :].astype(jnp.float32)
    amplitude = jnp.sqrt(real_part * real_part + imag_part * imag_part).astype(jnp.bfloat16)
    row_ids = lax.broadcasted_iota(jnp.int32, (bin_count, bin_count), 0)
    col_ids = lax.broadcasted_iota(jnp.int32, (bin_count, bin_count), 1)
    band_mask = jnp.abs(row_ids - col_ids) <= SMOOTH_HALF
    counts = jnp.sum(band_mask.astype(jnp.float32), axis=0)
    summed = jnp.dot(
        amplitude.reshape(-1, bin_count),
        band_mask.astype(jnp.bfloat16),
        preferred_element_type=jnp.float32,
    )
    smooth = summed.reshape(amplitude.shape) / counts
    scaling = valid_flags.astype(jnp.float32)[:, :, None] / (smooth + 1e-05)
    whitened = (spectra.astype(jnp.float32) * scaling[:, :, None, :]).astype(jnp.bfloat16)
    return jnp.transpose(whitened, (3, 2, 0, 1))


def cross_terms(owned, partner):
    rotated = jnp.stack([-partner[:, 1], partner[:, 0]], axis=1)
    joined = jnp.concatenate([partner, rotated], axis=3)
    return lax.dot_general(
        owned, joined, (((1, 2), (1, 2)), ((0,), (0,))), preferred_element_type=jnp.float32
    )


def invert(received, table, scaling):
    bin_count, rows_here, doubled = received.shape
    stack = received.astype(jnp.bfloat16).reshape(bin_count, rows_here, 2, doubled // 2)
    result = lax.dot_general(
        stack, table, (((0, 2), (0, 1)), ((), ())), preferred_element_type=jnp.float32
    )
    return (result * scaling).astype(jnp.bfloat16)


def shards_plain(spectra, valid_flags):
    seg_count = lax.axis_size("seg")
    windows_here = spectra.shape[0]
    bin_count = spectra.shape[3]
    table = lag_table(bin_count, LAG_COUNT)
    scaling = 1.0 / math.sqrt(windows_here * seg_count * bin_count)
    owned = whiten(spectra, valid_flags)
    previous_white = owned
    results = []
    for rounds_done in range(ROUNDS):
        stride = rounds_done + 1
        previous_white = passed_along(owned, "blk", stride)
        partials = cross_terms(owned, previous_white)
        received = lax.psum_scatter(
            partials.astype(jnp.bfloat16), "seg", scatter_dimension=1, tiled=True
        ).astype(jnp.float32)
        results.append(invert(received, table, scaling))
    return jnp.stack(results)


PIECES = 8
ROW_GROUP = 8
ROW_PAD = 8
MESH = pl.DeviceIdType.MESH


def exchange_kernel(blk_count, seg_count, own, gathered, own_all, transit, local_sem, near_send,
                    near_recv, seg_send, seg_recv):
    blk, seg = lax.axis_index("blk"), lax.axis_index("seg")
    place = lax.rem(blk, 4)
    low, high = lax.rem(place, 2), place // 2
    across_x = blk + 1 - 2 * low
    across_y = blk + 2 - 4 * high
    up_z = lax.rem(blk + 4, blk_count)
    down_z = lax.rem(blk + blk_count - 4, blk_count)
    siblings = [lax.rem(seg + k, seg_count) for k in range(1, seg_count)]
    bins = own.shape[0] // PIECES
    barrier = pltpu.get_barrier_semaphore()

    def greet(target_blk, target_seg):
        pl.semaphore_signal(barrier, inc=1, device_id=(target_blk, target_seg), device_id_type=MESH)

    greet(across_x, seg)
    greet(across_y, seg)
    for sibling in siblings:
        greet(blk, sibling)

    @pl.when(high == 1)
    def _():
        greet(up_z, seg)
        greet(down_z, seg)

    pl.semaphore_wait(barrier, 2 + len(siblings) + 2 * high)

    def part(k):
        return pl.ds(k * bins, bins)

    def near(src, dst, send_row, recv_row, k, target):
        return pltpu.make_async_remote_copy(
            src_ref=src, dst_ref=dst, send_sem=near_send.at[send_row, k],
            recv_sem=near_recv.at[recv_row, k], device_id=(target, seg), device_id_type=MESH)

    def own_x(k):
        return near(own.at[part(k)], gathered.at[0, seg, part(k)], 0, 0, k, across_x)

    def own_y(k):
        return near(own.at[part(k)], gathered.at[1, seg, part(k)], 1, 1, k, across_y)

    def own_z(k):
        return near(own.at[part(k)], transit.at[part(k)], 2, 2, k, up_z)

    def forward_y(k):
        return near(transit.at[part(k)], gathered.at[1, seg, part(k)], 3, 1, k, across_y)

    def forward_x(k):
        return near(gathered.at[1, seg, part(k)], gathered.at[0, seg, part(k)], 4, 0, k, across_x)

    def share(src, dst, row, k, n):
        return pltpu.make_async_remote_copy(
            src_ref=src, dst_ref=dst, send_sem=seg_send.at[row, k, n],
            recv_sem=seg_recv.at[row, k, n], device_id=(blk, siblings[n]), device_id_type=MESH)

    def share_round(r, k, n):
        piece = gathered.at[r, seg, part(k)]
        return share(piece, piece, r, k, n)

    def landed_round(r, k, n):
        piece = gathered.at[r, lax.rem(seg + seg_count - n - 1, seg_count), part(k)]
        return share(piece, piece, r, k, n)

    def share_own(k, n):
        return share(own.at[part(k)], own_all.at[seg, part(k)], 2, k, n)

    def landed_own(k, n):
        piece = own_all.at[lax.rem(seg + seg_count - n - 1, seg_count), part(k)]
        return share(piece, piece, 2, k, n)

    firsts = ((low == 0, own_x), (high == 0, own_y), (high == 1, own_z))

    def start_own(k):
        for condition, make in firsts:
            @pl.when(condition)
            def _(make=make):
                make(k).start()

    def wait_own(k):
        for condition, make in firsts:
            @pl.when(condition)
            def _(make=make):
                make(k).wait_send()

    start_own(0)
    start_own(1)
    local = pltpu.make_async_copy(own, own_all.at[seg], local_sem)
    local.start()
    for k in range(PIECES):
        for n in range(len(siblings)):
            share_own(k, n).start()
    for k in range(PIECES + 1):
        if k < PIECES:
            wait_own(k)
            if k + 2 < PIECES:
                start_own(k + 2)

            @pl.when(high == 1)
            def _():
                own_z(k).wait_recv()
                forward_y(k).start()

            own_y(k).wait_recv()

            @pl.when(low == 1)
            def _():
                forward_x(k).start()

            for n in range(len(siblings)):
                share_round(1, k, n).start()
        if k >= 1:
            own_x(k - 1).wait_recv()
            for n in range(len(siblings)):
                share_round(0, k - 1, n).start()
    for k in range(PIECES):
        @pl.when(high == 1)
        def _():
            forward_y(k).wait_send()

        @pl.when(low == 1)
        def _():
            forward_x(k).wait_send()

        for n in range(len(siblings)):
            for r in range(ROUNDS):
                share_round(r, k, n).wait_send()
                landed_round(r, k, n).wait_recv()
            share_own(k, n).wait_send()
            landed_own(k, n).wait_recv()
    local.wait()


def exchange(own, blk_count, seg_count):
    others = max(seg_count - 1, 1)
    anywhere = pl.BlockSpec(memory_space=pl.ANY)
    gathered, own_all, _ = pl.pallas_call(
        functools.partial(exchange_kernel, blk_count, seg_count),
        out_shape=(
            jax.ShapeDtypeStruct((ROUNDS, seg_count, *own.shape), own.dtype),
            jax.ShapeDtypeStruct((seg_count, *own.shape), own.dtype),
            jax.ShapeDtypeStruct(own.shape, own.dtype),
        ),
        in_specs=[anywhere],
        out_specs=(anywhere,) * 3,
        scratch_shapes=[
            pltpu.SemaphoreType.DMA,
            pltpu.SemaphoreType.DMA((5, PIECES)),
            pltpu.SemaphoreType.DMA((3, PIECES)),
            pltpu.SemaphoreType.DMA((3, PIECES, others)),
            pltpu.SemaphoreType.DMA((3, PIECES, others)),
        ],
        compiler_params=pltpu.CompilerParams(
            collective_id=0, has_side_effects=True, vmem_limit_bytes=60 * 2**20),
    )(own)
    return gathered, own_all


def folded_table(bin_count, lag_count):
    steps = np.outer(np.arange(bin_count) + BAND_START, np.arange(lag_count) - lag_count // 2) % WIN_SAMPLES
    angles = steps.astype(np.float32) * np.float32(2.0 * math.pi / WIN_SAMPLES)
    return jnp.asarray(np.concatenate([np.cos(angles), -np.sin(angles)]), jnp.bfloat16)


def correlate_kernel(chunk_count, scaling, own_ref, partner_ref, table_ref, out_ref, cross, left, turned):
    step = pl.program_id(1)
    segments, bins_here = own_ref.shape[:2]
    width = partner_ref.shape[-1]
    bin_count, rows, _ = turned.shape
    pitch = cross.shape[1] // bin_count
    group = out_ref.shape[1]

    @pl.when((step < chunk_count) & (pl.program_id(0) == 0))
    def _():
        mine = pl.ds(pl.multiple_of(lax.axis_index("seg") * rows, 16), rows)

        @pl.loop(0, bins_here, unroll=8)
        def _(f):
            stacked = jnp.concatenate(
                [own_ref[s, f, p] for p in range(2) for s in range(segments)], axis=0)
            left[pl.ds(0, width), pl.ds(0, stacked.shape[0])] = stacked.T
            turned[step * bins_here + f] = left[mine, pl.ds(0, stacked.shape[0])]

    @pl.when(step < chunk_count)
    def _():
        @pl.loop(0, bins_here, unroll=32)
        def _(f):
            real = jnp.concatenate([partner_ref[0, s, f, 0] for s in range(segments)], axis=0)
            imag = jnp.concatenate([partner_ref[0, s, f, 1] for s in range(segments)], axis=0)
            joined = jnp.concatenate(
                [jnp.concatenate([real, -imag], axis=1), jnp.concatenate([imag, real], axis=1)], axis=0)
            result = jnp.dot(
                turned[step * bins_here + f], joined, preferred_element_type=jnp.float32)
            start = pl.multiple_of((step * bins_here + f) * pitch, 8)
            cross[0, pl.ds(start, rows), :] = result[:, :width]
            cross[1, pl.ds(start, rows), :] = result[:, width:]

    @pl.when(step >= chunk_count)
    def _():
        first = (step - chunk_count) * group
        for n in range(group):
            for k in range(2):
                picked = cross[k, pl.ds(first + n, bin_count, stride=pitch), :]
                left[n * width:(n + 1) * width, k * bin_count:(k + 1) * bin_count] = (
                    picked.astype(jnp.bfloat16).T)
        lags = table_ref.shape[1]
        span = 256

        @pl.loop(0, lags // span, unroll=True)
        def _(c):
            columns = pl.ds(pl.multiple_of(c * span, span), span)
            result = jnp.dot(left[...], table_ref[:, columns], preferred_element_type=jnp.float32)
            out_ref[0, :, :, columns] = (result * scaling).astype(jnp.bfloat16).reshape(
                group, width, span)


def correlate(own, gathered, table, scaling):
    rounds, seg_count, bin_count, _, windows, width = gathered.shape
    rows, depth = width // seg_count, 2 * seg_count * windows
    lags = table.shape[1]
    bins_here = bin_count // 16
    chunk_count = bin_count // bins_here
    group = ROW_GROUP
    steps = chunk_count + rows // group
    return pl.pallas_call(
        functools.partial(correlate_kernel, chunk_count, scaling),
        grid=(rounds, steps),
        out_shape=jax.ShapeDtypeStruct((rounds, rows, width, lags), jnp.bfloat16),
        in_specs=[
            pl.BlockSpec((seg_count, bins_here, 2, windows, width),
                         lambda r, t: (0, jnp.where(r == 0, jnp.minimum(t, chunk_count - 1), chunk_count - 1), 0, 0, 0)),
            pl.BlockSpec((1, seg_count, bins_here, 2, windows, width),
                         lambda r, t: (r, 0, jnp.minimum(t, chunk_count - 1), 0, 0, 0)),
            pl.BlockSpec((2 * bin_count, lags), lambda r, t: (0, 0)),
        ],
        out_specs=pl.BlockSpec((1, group, width, lags),
                               lambda r, t: (r, jnp.maximum(t - chunk_count, 0), 0, 0)),
        scratch_shapes=[
            pltpu.VMEM((2, bin_count * (rows + ROW_PAD), width), jnp.float32),
            pltpu.VMEM((group * width, 2 * bin_count), jnp.bfloat16),
            pltpu.VMEM((bin_count, rows, depth), jnp.bfloat16),
        ],
        compiler_params=pltpu.CompilerParams(vmem_limit_bytes=60 * 2**20),
        cost_estimate=pl.CostEstimate(
            flops=4 * rounds * rows * width * bin_count * lags,
            bytes_accessed=2 * rounds * rows * width * lags, transcendentals=0),
    )(own, gathered, table)


def shards(spectra, valid_flags):
    seg_count, blk_count = lax.axis_size("seg"), lax.axis_size("blk")
    windows_here, width, _, bin_count = spectra.shape
    rows = width // seg_count
    fits = 2 * bin_count * rows * width * 4 <= 36 * 2**20
    if width != 128 or rows % 8 or blk_count % 4 or blk_count < 8 or bin_count % 128 or not fits:
        return shards_plain(spectra, valid_flags)
    scaling = 1.0 / math.sqrt(windows_here * seg_count * bin_count)
    table = folded_table(bin_count, LAG_COUNT)
    owned = whiten(spectra, valid_flags)
    padded = -(-windows_here // 16) * 16
    owned = jnp.pad(owned, ((0, 0), (0, 0), (0, padded - windows_here), (0, 0)))
    gathered, own_all = exchange(owned, blk_count, seg_count)
    return correlate(own_all, gathered, table, scaling)


def solution(mesh):
    in_specs = (P("seg", "blk", None, None), P("seg", "blk"))
    out_specs = P(None, ("blk", "seg"), None, None)
    return jax.shard_map(shards, mesh=mesh, in_specs=in_specs, out_specs=out_specs, check_vma=False)
```
